128 devices in a mesh: tx: 8 (over x, core), ty: 16 (over z, y).
Axes of the slice: x: 4, y: 4, z: 4, core: 2. Of those that a mesh axis runs over, the one named last changes fastest.
Arguments:
- solution: float32 [4, 1024, 4096], P(None, 'tx', 'ty'), may hold values from -6 to 6
- residual: float32 [4, 1024, 4096], P(None, 'tx', 'ty')
- direction: float32 [4, 1024, 4096], P(None, 'tx', 'ty')
- blocks: bfloat16 [32768, 128, 256], P(('tx', 'ty')), may hold values from -0.375 to 0.375
- bin_owner: int32 [32768, 1], P(('tx', 'ty')), may hold values from 0 to 127; in each aligned block of 256 rows (0 to 255, 256 to 511, ...) at most 3 rows name the same one
- bin_tile: int32 [32768], P(('tx', 'ty')), may hold values from 0 to 127
Outputs:
- next_solution: float32 [4, 1024, 4096], P(None, 'tx', 'ty')
- next_residual: float32 [4, 1024, 4096], P(None, 'tx', 'ty')
- next_direction: float32 [4, 1024, 4096], P(None, 'tx', 'ty')
The draws below stay inside these ranges and needn't reach their ends.
Inputs may be any that keep to these rules, and one draw needn't show every extreme that they name: `bin_owner`: among the bins of one device, at most 3 name the same owner, and on some devices some owner is named by exactly 3 of them.
All inputs are finite; a program needn't handle non-finite values.
Results may differ from the reference program's by a relative error of at most 0.0024.
Values may be sent and summed in bfloat16 or wider, within the bound.
A program may use at most 128 MiB of HBM per device.

```python
import math
import jax
import jax.numpy as jnp
import numpy as np
from jax import lax

BEACONS = 4
TILE_SIDE = 16
TILE_CELLS = 256
BIN_ROWS = 128
ROWS_DEV = 128
COLS_DEV = 256
BINS_DEV = 256
CAP = 3
TILES_DEV = 128
ROWS = 1024
COLS = 4096
BINS = 32768
N_TX = 8
N_TY = 16


def rough_field(key):
    keys = jax.random.split(key, 2)
    rows = jnp.arange(ROWS, dtype=jnp.float32)[:, None] / ROWS
    cols = jnp.arange(COLS, dtype=jnp.float32)[None, :] / COLS
    slope = jnp.exp(math.log(3.0) * (rows + cols)) / 3.0
    beacon = jax.random.uniform(keys[0], (BEACONS, 1, 1), minval=0.5, maxval=2.0)
    scale = slope[None, :, :] * beacon
    noise = jax.random.normal(keys[1], (BEACONS, ROWS, COLS), dtype=jnp.float32)
    return (scale * noise).astype(jnp.float32)


def draw_residual(key, part):
    return rough_field(jax.random.fold_in(key, 11))


def draw_direction(key, part):
    return rough_field(jax.random.fold_in(key, 23))


def set_ends(entries, rng, low, high):
    dims = entries.shape
    index_at = [jax.random.randint(jax.random.fold_in(rng, axis), (), 0, dims[axis]) for axis in range(len(dims))]
    entries = entries.at[tuple(index_at)].set(low)
    longest = dims.index(max(dims))
    index_at[longest] = (index_at[longest] + 1) % dims[longest]
    return entries.at[tuple(index_at)].set(high)


def shard_levels(stream_key, shape, cuts, least, high):
    loudness = 1.0
    for dim, blocks in cuts:
        heights = jax.random.uniform(jax.random.fold_in(jax.random.fold_in(stream_key, 6), dim), (blocks,), jnp.float32, least / len(cuts), high / len(cuts))
        loudness = loudness * jnp.repeat(jnp.exp(heights), shape[dim] // blocks).reshape((-1,) + (1,) * (len(shape) - 1 - dim))
    return loudness


def deal_out(own_key, own, number, rows, count, top, most, skew):
    ranking = jax.random.permutation(own_key, count)
    heavy_load, usual = load_shares(count, rows * top, most, skew, True), load_shares(count, rows * top, most, skew, False)
    places = jnp.arange(count)

    def named(sizes, offset_by):
        used = int((sizes > 0).sum())
        fixed = max(1, used // 4)
        passed = fixed + (places - fixed + offset_by * (used - fixed)) % max(1, count - fixed)
        return jnp.zeros((count,), jnp.int32).at[ranking[jnp.where(places < fixed, places, passed)]].set(jnp.asarray(sizes, jnp.int32))

    sizes = jnp.where(number % 4 == 0, named(heavy_load, number // 4), named(usual, number - number // 4 - 1))
    mixed = jax.random.permutation(jax.random.fold_in(own, 3), count)
    donor, sink = mixed[0:count // 2 * 2:2], mixed[1:count // 2 * 2:2]
    room = jnp.minimum(sizes[donor] - 1, most - sizes[sink]) // 2
    room = jnp.where((donor == ranking[0]) | (sink == ranking[0]) | (sizes[sink] == 0), 0, jnp.maximum(room, 0))
    passed = jax.random.randint(jax.random.fold_in(own, 4), (count // 2,), 0, 1 << 20) % (room + 1)
    sizes = sizes.at[donor].add(-passed).at[sink].add(passed)
    labels = jnp.searchsorted(jnp.cumsum(sizes), jnp.arange(rows * top), side="right").astype(jnp.int32)
    listing = labels.reshape(top, rows).T
    listing = listing[jax.random.permutation(jax.random.fold_in(own, 1), rows)]
    offset_by = jax.random.randint(jax.random.fold_in(own, 2), (rows, 1), 0, top)
    return jnp.take_along_axis(listing, (jnp.arange(top)[None, :] + offset_by) % top, axis=1)


def load_shares(number_of, total, bound, skew, full):
    portions = [(1 << 20) // math.isqrt(standing ** skew) + 1 for standing in range(1, number_of + 1)]
    largest = bound if full else min(bound, max(-(-total // number_of), total * portions[0] // sum(portions)))
    least = 1 if total - largest >= number_of - 1 else 0
    counts, surplus = [largest] + [least] * (number_of - 1), total - largest - least * (number_of - 1)
    while surplus > 0:
        candidates = [i for i in range(1, number_of) if counts[i] < largest] or [i for i in range(1, number_of) if counts[i] < bound]
        mass, left = sum([portions[i] for i in candidates]), surplus
        for i in candidates:
            more = min(bound - counts[i], max(1, left * portions[i] // mass), surplus)
            counts[i] = counts[i] + more
            surplus = surplus - more
    return np.array(counts)


def bell_draw(rng, dims, scale, bound, cuts=(), kind=jnp.bfloat16):
    values = scale * jax.random.normal(rng, dims, jnp.float32)
    if cuts:
        values = values * shard_levels(rng, dims, cuts, -0.22, 0.18)
    return jnp.clip(values, -bound, bound).astype(kind)


def setup_inputs(seed: int = 0) -> dict:
    arg_keys = jax.random.split(jax.random.key(seed), 7)
    solution = bell_draw(arg_keys[0], (BEACONS, ROWS, COLS), 1.0, 6.0, ((1, 8), (2, 16)), jnp.float32)
    residual = draw_residual(jax.random.fold_in(arg_keys[6], 71), 0)
    direction = draw_direction(jax.random.fold_in(arg_keys[6], 71), 0)
    blocks = bell_draw(arg_keys[3], (BINS, BIN_ROWS, TILE_CELLS), TILE_CELLS ** -0.5, 0.375, ((0, 128),))
    bin_owner_keys = jax.random.split(jax.random.fold_in(arg_keys[4], 1), BINS // BINS_DEV)
    bin_owner_turns = jax.random.permutation(jax.random.fold_in(arg_keys[4], 3), BINS // BINS_DEV)
    bin_owner = jax.vmap(lambda own, number: deal_out(jax.random.fold_in(arg_keys[4], 2), own, number, BINS_DEV, N_TX * N_TY, 1, CAP, 2))(bin_owner_keys, bin_owner_turns).reshape((BINS, 1))
    bin_tile = set_ends(jax.random.randint(arg_keys[5], (BINS,), 0, TILES_DEV), jax.random.fold_in(arg_keys[5], 1), 0, TILES_DEV - 1).astype(jnp.int32)
    return dict(solution=solution, residual=residual, direction=direction, blocks=blocks, bin_owner=bin_owner, bin_tile=bin_tile)


smooth_weight = 0.25


def laplace(field):
    padded = jnp.pad(field, ((0, 0), (1, 1), (1, 1)))
    near = padded[:, 2:, 1:-1] + padded[:, :-2, 1:-1] + padded[:, 1:-1, 2:] + padded[:, 1:-1, :-2]
    return 4.0 * field - near


def split_tiles(field):
    across = ROWS_DEV // TILE_SIDE
    down = COLS_DEV // TILE_SIDE
    shaped = field.reshape(BEACONS, N_TX, across, TILE_SIDE, N_TY, down, TILE_SIDE)
    shaped = shaped.transpose(1, 4, 2, 5, 0, 3, 6)
    return shaped.reshape(N_TX * N_TY * across * down, BEACONS, TILE_SIDE * TILE_SIDE)


def join_tiles(tiles):
    across = ROWS_DEV // TILE_SIDE
    down = COLS_DEV // TILE_SIDE
    shaped = tiles.reshape(N_TX, N_TY, across, down, BEACONS, TILE_SIDE, TILE_SIDE)
    shaped = shaped.transpose(4, 0, 2, 5, 1, 3, 6)
    return shaped.reshape(BEACONS, ROWS_DEV * N_TX, COLS_DEV * N_TY)


def reference(solution, residual, direction, blocks, bin_owner, bin_tile):
    devices = N_TX * N_TY
    tiles_dev = (ROWS_DEV // TILE_SIDE) * (COLS_DEV // TILE_SIDE)
    rounded = split_tiles(direction.astype(jnp.bfloat16))
    places = (bin_owner[:, 0] * tiles_dev + bin_tile).astype(jnp.int32)
    weights = blocks.reshape(devices, BINS_DEV, BIN_ROWS, TILE_CELLS)
    places = places.reshape(devices, BINS_DEV)

    def add_device(total, item):
        block, rows_at = item
        picked = rounded[rows_at].astype(jnp.float32)
        wide = block.astype(jnp.float32)
        samples = jnp.einsum("bsc,bkc->bks", wide, picked).astype(jnp.bfloat16)
        adjoint = jnp.einsum("bsc,bks->bkc", wide, samples.astype(jnp.float32))
        return total.at[rows_at].add(adjoint), None

    total, _ = lax.scan(add_device, jnp.zeros(rounded.shape, jnp.float32), (weights, places))
    image = join_tiles(total) + smooth_weight * laplace(direction)
    norm_old = jnp.sum(residual * residual, axis=(1, 2))
    curvature = jnp.sum(direction * image, axis=(1, 2))
    alpha = (norm_old / curvature)[:, None, None]
    next_solution = solution + alpha * direction
    next_residual = residual - alpha * image
    norm_new = jnp.sum(next_residual * next_residual, axis=(1, 2))
    next_direction = next_residual + (norm_new / norm_old)[:, None, None] * direction
    return next_solution, next_residual, next_direction
```

```python
import functools

import jax
import jax.numpy as jnp
from jax import lax
from jax.experimental import pallas as pl
from jax.experimental.pallas import tpu as pltpu
from jax.sharding import PartitionSpec as P

SIDE = 16
CAP = 3
GROUP = 8
SMOOTH = 0.25
MESH = pl.DeviceIdType.MESH
F32 = jnp.float32
BF16 = jnp.bfloat16
NT = (((1,), (1,)), ((), ()))
NN = (((1,), (0,)), ((), ()))


def swap_blocks(regs, lane):
    for j in (4, 2, 1):
        low = ((lane >> 4) & j) == 0
        made = list(regs)
        for r in range(8):
            if r & j == 0:
                a, b = regs[r], regs[r + j]
                made[r] = jnp.where(low, a, pltpu.roll(b, 16 * j, 1))
                made[r + j] = jnp.where(low, pltpu.roll(a, 128 - 16 * j, 1), b)
        regs = made
    return regs


def fold(x):
    rows, cols = x.shape
    y = x.reshape(rows // 8, 8, cols).sum(axis=0)
    return sum(y[:, c : c + 128] for c in range(0, cols, 128))


def fold_max(x):
    rows, cols = x.shape
    y = x.reshape(rows // 8, 8, cols).max(axis=0)
    out = y[:, :128]
    for c in range(128, cols, 128):
        out = jnp.maximum(out, y[:, c : c + 128])
    return out


def kernel(
    nx,
    ny,
    owner_ref,
    tile_ref,
    dir_ref,
    res_ref,
    blocks_ref,
    image_ref,
    coef_ref,
    bl,
    t1,
    t2,
    own,
    sb,
    fetched,
    ret,
    arrived,
    acc_ref,
    fld,
    til,
    hr,
    hrin,
    hc,
    hcin,
    bins_v,
    want_v,
    s1,
    s2,
    bins_s,
    want_s,
    sem_bl,
    sem_loc,
    sem_req,
    sem_halo,
    sem_dir,
    sem_ret,
    sem_send,
    sem_red,
):
    n = nx * ny
    beacons, rows, cols = dir_ref.shape
    count = owner_ref.shape[1]
    groups = n // GROUP
    tx, ty = lax.axis_index("tx"), lax.axis_index("ty")

    def ahead(k):
        return lax.rem(tx + k // ny, nx), lax.rem(ty + k % ny, ny)

    def behind(k):
        return lax.rem(tx + nx - k // ny, nx), lax.rem(ty + ny - k % ny, ny)

    def send(src, dst, send_sem, recv_sem, device):
        pltpu.make_async_remote_copy(
            src_ref=src,
            dst_ref=dst,
            send_sem=send_sem,
            recv_sem=recv_sem,
            device_id=device,
            device_id_type=MESH,
        ).start()

    def drain(ref, sem):
        pltpu.make_async_copy(ref, ref, sem).wait()

    blocks_copy = pltpu.make_async_copy(blocks_ref, bl, sem_bl)
    blocks_copy.start()

    barrier = pltpu.get_barrier_semaphore()
    for a in range(1, nx):
        pl.semaphore_signal(barrier, inc=1, device_id=(lax.rem(tx + a, nx), ty), device_id_type=MESH)
    for b in range(1, ny):
        pl.semaphore_signal(barrier, inc=1, device_id=(tx, lax.rem(ty + b, ny)), device_id_type=MESH)

    lane = lax.broadcasted_iota(jnp.int32, (8, 128), 1)
    row = lax.broadcasted_iota(jnp.int32, (8, 128), 0)

    with jax.named_scope("requests"):
        owner = owner_ref[...]
        ox, oy = owner // ny, lax.rem(owner, ny)
        dx, dy = ox - tx, oy - ty
        rel = jnp.where(dx < 0, dx + nx, dx) * ny + jnp.where(dy < 0, dy + ny, dy)
        member = rel == lax.broadcasted_iota(jnp.int32, (128, count), 0)
        earlier = lax.broadcasted_iota(jnp.int32, (count, count), 0) < lax.broadcasted_iota(
            jnp.int32, (count, count), 1
        )
        before = lax.dot_general(
            member.astype(F32).astype(BF16),
            earlier.astype(F32).astype(BF16),
            NN,
            preferred_element_type=F32,
        )
        told = lax.broadcasted_iota(jnp.int32, (16, count), 0)
        bin_no = lax.broadcasted_iota(jnp.int32, (16, count), 1)
        payload = jnp.where(told < 8, tile_ref[...] + 1, bin_no + 1).astype(F32)
        slots = jnp.zeros((16, 128), F32)
        for r in range(CAP):
            chosen = jnp.where(member, jnp.where(before == float(r), 1.0, 0.0), 0.0).astype(BF16)
            mine = jnp.where((told & 7) == r, payload, 0.0).astype(BF16)
            slots += lax.dot_general(mine, chosen, NT, preferred_element_type=F32)
        slots = slots - 1.0
        bins_v[...] = jnp.maximum(slots[8:], 0.0).astype(jnp.int32)
        bins_copy = pltpu.make_async_copy(bins_v, bins_s, sem_loc.at[0])
        bins_copy.start()

        table = jnp.where(row < CAP, slots[:8], 0.0)
        for b in range(beacons):
            norm = jnp.sum(fold(res_ref[b] * res_ref[b]), axis=0, keepdims=True)
            table = jnp.where(row == 4 + b, norm, table)
            high = jnp.max(fold_max(jnp.abs(dir_ref[b])), axis=0, keepdims=True)
            high = jnp.broadcast_to(high, (8, 128))
            high = jnp.maximum(high, pltpu.roll(high, 64, 1))
            high = jnp.maximum(high, pltpu.roll(high, 32, 1))
            table = jnp.where((row == 3) & ((lane >> 5) == b), high, table)
        t1[0] = table

    columns = jnp.zeros((rows, 128), F32)
    lane_r = lax.broadcasted_iota(jnp.int32, (rows, 128), 1)
    for b in range(beacons):
        hr[b : b + 1, :] = dir_ref[b, 0:1, :]
        hr[4 + b : 5 + b, :] = dir_ref[b, rows - 1 : rows, :]
        columns = jnp.where(lane_r == b, dir_ref[b, :, 0:1], columns)
        columns = jnp.where(lane_r == 4 + b, dir_ref[b, :, cols - 1 : cols], columns)
    hc[...] = columns.T[:8]

    pl.semaphore_wait(barrier, nx - 1 + ny - 1)

    for a in range(1, nx):
        send(t1.at[0], t1.at[a], sem_req.at[0], sem_req.at[1], (lax.rem(tx + a, nx), ty))
    send(hr, hrin.at[0], sem_halo.at[4], sem_halo.at[0], (lax.rem(tx + nx - 1, nx), ty))
    send(hr, hrin.at[1], sem_halo.at[5], sem_halo.at[1], (lax.rem(tx + 1, nx), ty))
    send(hc, hcin.at[0], sem_halo.at[6], sem_halo.at[2], (tx, lax.rem(ty + ny - 1, ny)))
    send(hc, hcin.at[1], sem_halo.at[7], sem_halo.at[3], (tx, lax.rem(ty + 1, ny)))

    with jax.named_scope("tiles"):
        for b in range(beacons):
            for s in range(rows // 8):
                at = (s // 2) * 64 + (s % 2) * 32 + b * 8
                for half in range(2):
                    fld[half, at : at + 8, :] = dir_ref[b, s * 8 : s * 8 + 8, half * 128 : half * 128 + 128]

        def cut(ti, carry):
            for half in range(2):
                regs = [fld[half, pl.ds(ti * 64 + r, 8, stride=8), :] for r in range(8)]
                for q, reg in enumerate(swap_blocks(regs, lane)):
                    own[ti * 16 + half * 8 + q] = reg.astype(BF16)
            return carry

        lax.fori_loop(0, rows // SIDE, cut, 0)

    def combine(tables, place, total):
        asked, high, summed = tables[0], tables[0], tables[0]
        for i in range(1, total):
            asked = jnp.where(place == i, tables[i], asked)
            high = jnp.maximum(high, tables[i])
            summed = summed + tables[i]
        return jnp.where(row < CAP, asked, jnp.where(row == CAP, high, summed))

    drain(t1.at[pl.ds(1, nx - 1)], sem_req.at[1])
    t2[0] = combine(t1, lane // ny, nx)
    for b in range(1, ny):
        send(t2.at[0], t2.at[b], sem_req.at[2], sem_req.at[3], (tx, lax.rem(ty + b, ny)))
    drain(t2.at[pl.ds(1, ny - 1)], sem_req.at[3])
    table = combine(t2, lax.rem(lane, ny), ny)
    want_v[...] = jnp.maximum(table, 0.0).astype(jnp.int32)
    want_copy = pltpu.make_async_copy(want_v, want_s, sem_loc.at[1])
    want_copy.start()
    want_copy.wait()

    with jax.named_scope("serve"):

        def serve(g, carry):
            for i in range(GROUP):
                k = g * GROUP + i
                for r in range(CAP):
                    sb[k, r] = own[jnp.clip(want_s[r, k], 0, own.shape[0] - 1)]

                def far():
                    send(sb.at[k], fetched.at[k], sem_send.at[0], sem_dir.at[g], behind(k))

                def near():
                    pltpu.make_async_copy(sb.at[k], fetched.at[k], sem_dir.at[g]).start()

                if i == 0:
                    pl.when(g == 0)(near)
                    pl.when(g > 0)(far)
                else:
                    far()
            return carry

        lax.fori_loop(0, groups, serve, 0)

    with jax.named_scope("laplace"):
        for i in range(2):
            drain(hrin.at[i], sem_halo.at[i])
            drain(hcin.at[i], sem_halo.at[2 + i])
        below = jnp.where(tx == nx - 1, 0.0, hrin[0])
        above = jnp.where(tx == 0, 0.0, hrin[1])
        right = jnp.where(ty == ny - 1, 0.0, hcin[0])
        left = jnp.where(ty == 0, 0.0, hcin[1])
        side = jnp.where(row < 4, right, left)
        side = jnp.concatenate([side, jnp.zeros((120, 128), F32)], axis=0).T
        row_f = lax.broadcasted_iota(jnp.int32, (rows, cols), 0)
        col_f = lax.broadcasted_iota(jnp.int32, (rows, cols), 1)
        for b in range(beacons):
            d = dir_ref[b]
            up = jnp.where(row_f == 0, above[4 + b : 5 + b], pltpu.roll(d, 1, 0))
            down = jnp.where(row_f == rows - 1, below[b : b + 1], pltpu.roll(d, rows - 1, 0))
            west = jnp.where(col_f == 0, side[:rows, 4 + b : 5 + b], pltpu.roll(d, 1, 1))
            east = jnp.where(col_f == cols - 1, side[:rows, b : b + 1], pltpu.roll(d, cols - 1, 1))
            image_ref[b] = SMOOTH * (4.0 * d - (down + up + east + west))

    bins_copy.wait()
    blocks_copy.wait()

    low = row < 4

    def products(g, carry):
        drain(fetched.at[pl.ds(g * GROUP, GROUP)], sem_dir.at[g])
        spots = [(g * GROUP + i // CAP, i % CAP) for i in range(GROUP * CAP)]
        ids = [jnp.clip(bins_s[r, k], 0, count - 1) for k, r in spots]
        parts = []
        for i in range(0, GROUP * CAP, 2):
            (kx, rx), (ky, ry) = spots[i : i + 2]
            x, y = fetched[kx, rx].astype(F32), fetched[ky, ry].astype(F32)
            first = jnp.where(low, x, pltpu.roll(y, 4, 0))
            second = jnp.where(low, pltpu.roll(x, 4, 0), y)
            parts.append(jnp.concatenate([first, second], axis=1))
        parts += [jnp.zeros((8, 256), F32)] * ((128 - 4 * GROUP * CAP) // 8)
        picked = jnp.concatenate(parts, axis=0).astype(BF16)
        held = None
        for i in range(GROUP * CAP):
            part = lax.dot_general(bl[ids[i]], picked, NT, preferred_element_type=F32).reshape(16, 8, 128)
            held = part if held is None else jnp.where(((lane >> 2) == i)[None], part, held)
        samples = held.reshape(128, 128).T.astype(BF16)
        for i in range(0, GROUP * CAP, 2):
            pair = samples[i * 4 : i * 4 + 8]
            x = lax.dot_general(pair, bl[ids[i]], NN, preferred_element_type=F32)
            y = lax.dot_general(pair, bl[ids[i + 1]], NN, preferred_element_type=F32)
            (kx, rx), (ky, ry) = spots[i : i + 2]
            ret[kx, rx] = jnp.where(low, x[:, :128], pltpu.roll(x[:, 128:], 4, 0)).astype(BF16)
            ret[ky, ry] = jnp.where(low, pltpu.roll(y[:, :128], 4, 0), y[:, 128:]).astype(BF16)
        for i in range(GROUP):
            k = g * GROUP + i

            def far():
                send(ret.at[k], arrived.at[k], sem_send.at[1], sem_ret.at[g], ahead(k))

            def near():
                pltpu.make_async_copy(ret.at[k], arrived.at[k], sem_ret.at[g]).start()

            if i == 0:
                pl.when(g == 0)(near)
                pl.when(g > 0)(far)
            else:
                far()
        return carry

    with jax.named_scope("products"):
        lax.fori_loop(0, groups, products, 0)

    with jax.named_scope("gather_up"):

        def widen(g, carry):
            drain(arrived.at[pl.ds(g * GROUP, GROUP)], sem_ret.at[g])
            for i in range(GROUP):
                for r in range(CAP):
                    at = pl.multiple_of((g * GROUP + i) * 8 * CAP + r * 8, 8)
                    acc_ref[pl.ds(at, 8), :] = arrived[g * GROUP + i, r].astype(F32)
            return carry

        lax.fori_loop(0, groups, widen, 0)

    with jax.named_scope("add_up"):
        number = lax.broadcasted_iota(jnp.int32, (128, n), 0).astype(F32)
        hits = jnp.concatenate(
            [jnp.where(number == table[r : r + 1, :n], 1.0, 0.0).astype(BF16) for r in range(CAP)], axis=1
        )
        for j in range(8):
            terms = jnp.concatenate(
                [acc_ref[pl.ds(r * 8 + j, n, stride=8 * CAP), :].astype(BF16) for r in range(CAP)], axis=0
            )
            til[pl.ds(j, 128, stride=8), :] = lax.dot_general(hits, terms, NN, preferred_element_type=F32)

        def paste(ti, carry):
            for half in range(2):
                regs = []
                for q in range(8):
                    at = pl.multiple_of((ti * 16 + half * 8 + q) * 8, 8)
                    regs.append(til[pl.ds(at, 8), :])
                for r, reg in enumerate(swap_blocks(regs, lane)):
                    fld[half, pl.ds(ti * 64 + r, 8, stride=8), :] = reg
            return carry

        lax.fori_loop(0, rows // SIDE, paste, 0)

    with jax.named_scope("sums"):
        first = jnp.zeros((8, 128), F32)
        second = jnp.zeros((8, 128), F32)
        scales = []
        for b in range(beacons):
            top = jnp.max(jnp.where((lane >> 5) == b, jnp.broadcast_to(table[3:4], (8, 128)), 0.0), axis=1, keepdims=True)
            top = jnp.maximum(jnp.broadcast_to(top, (8, 128)), 1e-30)
            scales.append(top)
            inverse = 1.0 / top
            dq = jnp.zeros((8, 128), F32)
            rq = jnp.zeros((8, 128), F32)
            qq = jnp.zeros((8, 128), F32)
            for s in range(rows // 8):
                at = (s // 2) * 64 + (s % 2) * 32 + b * 8
                for half in range(2):
                    span = (b, slice(s * 8, s * 8 + 8), slice(half * 128, half * 128 + 128))
                    q = fld[half, at : at + 8, :] + image_ref[span]
                    image_ref[span] = q
                    dq += dir_ref[span] * q
                    q = q * inverse
                    rq += res_ref[span] * q
                    qq += q * q
            dq = jnp.sum(dq, axis=0, keepdims=True)
            rq = jnp.sum(rq, axis=0, keepdims=True)
            qq = jnp.sum(qq, axis=0, keepdims=True)
            dq = jnp.broadcast_to(dq, (8, 128))
            rq = jnp.broadcast_to(rq, (8, 128))
            both = jnp.where(lane < 64, dq + pltpu.roll(dq, 64, 1), rq + pltpu.roll(rq, 64, 1))
            first = jnp.where(row == b, both, first)
            second = jnp.where(row == 4 + b, qq, second)
        s1[0] = jnp.where(row < 4, first, second)

    with jax.named_scope("reduce"):
        for b in range(1, ny):
            send(s1.at[0], s1.at[b], sem_red.at[0], sem_red.at[1], (tx, lax.rem(ty + b, ny)))
        drain(s1.at[pl.ds(1, ny - 1)], sem_red.at[1])
        total = s1[0]
        for b in range(1, ny):
            total = total + s1[b]
        s2[0] = total
        for a in range(1, nx):
            send(s2.at[0], s2.at[a], sem_red.at[2], sem_red.at[3], (lax.rem(tx + a, nx), ty))
        drain(s2.at[pl.ds(1, nx - 1)], sem_red.at[3])
        total = s2[0]
        for a in range(1, nx):
            total = total + s2[a]

        def whole(x):
            return jnp.broadcast_to(jnp.sum(x, axis=1, keepdims=True), (8, 128))

        norm_old = pltpu.roll(whole(table), 4, 0)
        curvature = whole(jnp.where(lane < 64, total, 0.0))
        cross = whole(jnp.where(lane < 64, 0.0, total))
        square = pltpu.roll(whole(total), 4, 0)
        top = scales[0]
        for b in range(1, beacons):
            top = jnp.where(row == b, scales[b], top)
        alpha = norm_old / curvature
        step = alpha * top
        norm_new = jnp.maximum(norm_old - 2.0 * step * cross + step * step * square, 0.0)
        beta = norm_new / norm_old
        coef_ref[...] = jnp.where(row < 4, alpha, pltpu.roll(beta, 4, 0))

    drain(t1.at[pl.ds(1, nx - 1)], sem_req.at[0])
    drain(t2.at[pl.ds(1, ny - 1)], sem_req.at[2])
    for i in range(2):
        drain(hr, sem_halo.at[4 + i])
        drain(hc, sem_halo.at[6 + i])
    drain(sb.at[pl.ds(1, n - 1)], sem_send.at[0])
    drain(ret.at[pl.ds(1, n - 1)], sem_send.at[1])
    drain(s1.at[pl.ds(1, ny - 1)], sem_red.at[0])
    drain(s2.at[pl.ds(1, nx - 1)], sem_red.at[2])


def per_device(nx, ny, solution, residual, direction, blocks, bin_owner, bin_tile):
    n = nx * ny
    beacons, rows, cols = direction.shape
    count = blocks.shape[0]
    vmem = pl.BlockSpec(memory_space=pltpu.VMEM)
    groups = n // GROUP
    slots = (n, CAP, 8, 128)
    image, coef = pl.pallas_call(
        functools.partial(kernel, nx, ny),
        out_shape=(
            jax.ShapeDtypeStruct(direction.shape, F32),
            jax.ShapeDtypeStruct((8, 128), F32),
        ),
        in_specs=[vmem] * 4 + [pl.BlockSpec(memory_space=pl.ANY)],
        out_specs=(vmem, vmem),
        scratch_shapes=[
            pltpu.VMEM(blocks.shape, BF16),
            pltpu.VMEM((nx, 8, 128), F32),
            pltpu.VMEM((ny, 8, 128), F32),
            pltpu.VMEM((128, 8, 128), BF16),
            pltpu.VMEM(slots, BF16),
            pltpu.VMEM(slots, BF16),
            pltpu.VMEM(slots, BF16),
            pltpu.VMEM(slots, BF16),
            pltpu.VMEM(((n + 1) * CAP * 8, 128), F32),
            pltpu.VMEM((2, beacons * rows + 8, 128), F32),
            pltpu.VMEM((1032, 128), F32),
            pltpu.VMEM((8, cols), F32),
            pltpu.VMEM((2, 8, cols), F32),
            pltpu.VMEM((8, 128), F32),
            pltpu.VMEM((2, 8, 128), F32),
            pltpu.VMEM((8, 128), jnp.int32),
            pltpu.VMEM((8, 128), jnp.int32),
            pltpu.VMEM((ny, 8, 128), F32),
            pltpu.VMEM((nx, 8, 128), F32),
            pltpu.SMEM((8, 128), jnp.int32),
            pltpu.SMEM((8, 128), jnp.int32),
            pltpu.SemaphoreType.DMA,
            pltpu.SemaphoreType.DMA((2,)),
            pltpu.SemaphoreType.DMA((4,)),
            pltpu.SemaphoreType.DMA((8,)),
            pltpu.SemaphoreType.DMA((groups,)),
            pltpu.SemaphoreType.DMA((groups,)),
            pltpu.SemaphoreType.DMA((2,)),
            pltpu.SemaphoreType.DMA((4,)),
        ],
        compiler_params=pltpu.CompilerParams(
            collective_id=0, has_side_effects=True, vmem_limit_bytes=48 * 2**20
        ),
        cost_estimate=pl.CostEstimate(
            flops=4 * count * 128 * 256 * 4, bytes_accessed=blocks.size * 2, transcendentals=0
        ),
        name="radio_map",
    )(bin_owner.reshape(1, count), bin_tile.reshape(1, count), direction, residual, blocks)
    alpha = coef[:4, 0][:, None, None]
    beta = coef[4:, 0][:, None, None]
    next_residual = residual - alpha * image
    next_solution = solution + alpha * direction
    next_direction = next_residual + beta * direction
    return next_solution, next_residual, next_direction


def solution(mesh):
    field = P(None, "tx", "ty")
    return jax.shard_map(
        functools.partial(per_device, mesh.shape["tx"], mesh.shape["ty"]),
        mesh=mesh,
        in_specs=(field, field, field, P(("tx", "ty"), None, None), P(("tx", "ty"), None), P(("tx", "ty"))),
        out_specs=(field, field, field),
        check_vma=False,
    )
```

```python
import functools

import jax
import jax.numpy as jnp
from jax import lax
from jax.experimental import pallas as pl
from jax.experimental.pallas import tpu as pltpu
from jax.sharding import PartitionSpec as P

SIDE = 16
CAP = 3
GROUP = 8
SMOOTH = 0.25
MESH = pl.DeviceIdType.MESH
F32 = jnp.float32
BF16 = jnp.bfloat16
NT = (((1,), (1,)), ((), ()))
NN = (((1,), (0,)), ((), ()))


def swap_blocks(regs, lane):
    for j in (4, 2, 1):
        low = ((lane >> 4) & j) == 0
        made = list(regs)
        for r in range(8):
            if r & j == 0:
                a, b = regs[r], regs[r + j]
                made[r] = jnp.where(low, a, pltpu.roll(b, 16 * j, 1))
                made[r + j] = jnp.where(low, pltpu.roll(a, 128 - 16 * j, 1), b)
        regs = made
    return regs


def fold(x):
    rows, cols = x.shape
    y = x.reshape(rows // 8, 8, cols).sum(axis=0)
    return sum(y[:, c : c + 128] for c in range(0, cols, 128))


def fold_max(x):
    rows, cols = x.shape
    y = x.reshape(rows // 8, 8, cols).max(axis=0)
    out = y[:, :128]
    for c in range(128, cols, 128):
        out = jnp.maximum(out, y[:, c : c + 128])
    return out


def kernel(
    nx,
    ny,
    bins_hbm,
    dir_hbm,
    res_hbm,
    blocks_ref,
    image_ref,
    coef_ref,
    bins_ref,
    dir_ref,
    res_ref,
    bl,
    t1,
    t2,
    own,
    sb,
    fetched,
    ret,
    arrived,
    acc_ref,
    fld,
    til,
    hr,
    hrin,
    hc,
    hcin,
    bins_v,
    want_v,
    s1,
    bins_s,
    want_s,
    sem_bl,
    sem_loc,
    sem_req,
    sem_halo,
    sem_dir,
    sem_ret,
    sem_send,
    sem_red,
):
    n = nx * ny
    beacons, rows, cols = dir_ref.shape
    count = bins_ref.shape[1]
    groups = n // GROUP
    tx, ty = lax.axis_index("tx"), lax.axis_index("ty")

    def place(g, i):
        if ny % GROUP == 0:
            return lax.div(g * GROUP, ny), lax.rem(g * GROUP, ny) + i
        return lax.div(g * GROUP + i, ny), lax.rem(g * GROUP + i, ny)

    def ahead(g, i):
        a, b = place(g, i)
        x, y = tx + a, ty + b
        return jnp.where(x >= nx, x - nx, x), jnp.where(y >= ny, y - ny, y)

    def behind(g, i):
        a, b = place(g, i)
        x, y = tx - a, ty - b
        return jnp.where(x < 0, x + nx, x), jnp.where(y < 0, y + ny, y)

    def send(src, dst, send_sem, recv_sem, device):
        pltpu.make_async_remote_copy(
            src_ref=src,
            dst_ref=dst,
            send_sem=send_sem,
            recv_sem=recv_sem,
            device_id=device,
            device_id_type=MESH,
        ).start()

    def drain(ref, sem):
        pltpu.make_async_copy(ref, ref, sem).wait()

    loads = [
        pltpu.make_async_copy(src, dst, sem_loc.at[2 + i])
        for i, (src, dst) in enumerate(
            ((bins_hbm, bins_ref), (dir_hbm, dir_ref), (res_hbm, res_ref))
        )
    ]
    for load in loads:
        load.start()
    blocks_copy = pltpu.make_async_copy(blocks_ref, bl, sem_bl)
    blocks_copy.start()

    barrier = pltpu.get_barrier_semaphore()
    for a in range(1, nx):
        pl.semaphore_signal(barrier, inc=1, device_id=(lax.rem(tx + a, nx), ty), device_id_type=MESH)
    for b in range(1, ny):
        pl.semaphore_signal(barrier, inc=1, device_id=(tx, lax.rem(ty + b, ny)), device_id_type=MESH)

    lane = lax.broadcasted_iota(jnp.int32, (8, 128), 1)
    row = lax.broadcasted_iota(jnp.int32, (8, 128), 0)

    with jax.named_scope("requests"):
        loads[0].wait()
        owner, tile = bins_ref[...] >> 7, bins_ref[...] & 127
        ox, oy = owner // ny, lax.rem(owner, ny)
        dx, dy = ox - tx, oy - ty
        rel = jnp.where(dx < 0, dx + nx, dx) * ny + jnp.where(dy < 0, dy + ny, dy)
        member = rel == lax.broadcasted_iota(jnp.int32, (128, count), 0)
        earlier = lax.broadcasted_iota(jnp.int32, (count, count), 0) < lax.broadcasted_iota(
            jnp.int32, (count, count), 1
        )
        before = lax.dot_general(
            member.astype(F32).astype(BF16),
            earlier.astype(F32).astype(BF16),
            NN,
            preferred_element_type=F32,
        )
        told = lax.broadcasted_iota(jnp.int32, (16, count), 0)
        bin_no = lax.broadcasted_iota(jnp.int32, (16, count), 1)
        payload = jnp.where(told < 8, tile + 1, bin_no + 1).astype(F32)
        slots = jnp.zeros((16, 128), F32)
        for r in range(CAP):
            chosen = jnp.where(member, jnp.where(before == float(r), 1.0, 0.0), 0.0).astype(BF16)
            mine = jnp.where((told & 7) == r, payload, 0.0).astype(BF16)
            slots += lax.dot_general(mine, chosen, NT, preferred_element_type=F32)
        slots = slots - 1.0
        bins_v[...] = jnp.maximum(slots[8:], 0.0).astype(jnp.int32)
        bins_copy = pltpu.make_async_copy(bins_v, bins_s, sem_loc.at[0])
        bins_copy.start()

        table = jnp.where(row < CAP, slots[:8], 0.0)
        loads[1].wait()
        loads[2].wait()
        for b in range(beacons):
            norm = jnp.sum(fold(res_ref[b] * res_ref[b]), axis=0, keepdims=True)
            table = jnp.where(row == 4 + b, norm, table)
            high = jnp.max(fold_max(jnp.abs(dir_ref[b])), axis=0, keepdims=True)
            high = jnp.broadcast_to(high, (8, 128))
            high = jnp.maximum(high, pltpu.roll(high, 64, 1))
            high = jnp.maximum(high, pltpu.roll(high, 32, 1))
            table = jnp.where((row == 3) & ((lane >> 5) == b), high, table)
        t1[0] = table

    columns = jnp.zeros((rows, 128), F32)
    lane_r = lax.broadcasted_iota(jnp.int32, (rows, 128), 1)
    for b in range(beacons):
        hr[b : b + 1, :] = dir_ref[b, 0:1, :]
        hr[4 + b : 5 + b, :] = dir_ref[b, rows - 1 : rows, :]
        columns = jnp.where(lane_r == b, dir_ref[b, :, 0:1], columns)
        columns = jnp.where(lane_r == 4 + b, dir_ref[b, :, cols - 1 : cols], columns)
    hc[...] = columns.T[:8]

    pl.semaphore_wait(barrier, nx - 1 + ny - 1)

    for a in range(1, nx):
        send(t1.at[0], t1.at[a], sem_req.at[0], sem_req.at[1], (lax.rem(tx + a, nx), ty))
    send(hr, hrin.at[0], sem_halo.at[4], sem_halo.at[0], (lax.rem(tx + nx - 1, nx), ty))
    send(hr, hrin.at[1], sem_halo.at[5], sem_halo.at[1], (lax.rem(tx + 1, nx), ty))
    send(hc, hcin.at[0], sem_halo.at[6], sem_halo.at[2], (tx, lax.rem(ty + ny - 1, ny)))
    send(hc, hcin.at[1], sem_halo.at[7], sem_halo.at[3], (tx, lax.rem(ty + 1, ny)))

    with jax.named_scope("tiles"):
        for b in range(beacons):
            for s in range(rows // 8):
                at = (s // 2) * 64 + (s % 2) * 32 + b * 8
                for half in range(2):
                    fld[half, at : at + 8, :] = dir_ref[b, s * 8 : s * 8 + 8, half * 128 : half * 128 + 128]

        def cut(ti, carry):
            for half in range(2):
                regs = [fld[half, pl.ds(ti * 64 + r, 8, stride=8), :] for r in range(8)]
                for q, reg in enumerate(swap_blocks(regs, lane)):
                    own[ti * 16 + half * 8 + q] = reg.astype(BF16)
            return carry

        lax.fori_loop(0, rows // SIDE, cut, 0)

    def combine(tables, place, total):
        asked, high, summed = tables[0], tables[0], tables[0]
        for i in range(1, total):
            asked = jnp.where(place == i, tables[i], asked)
            high = jnp.maximum(high, tables[i])
            summed = summed + tables[i]
        return jnp.where(row < CAP, asked, jnp.where(row == CAP, high, summed))

    drain(t1.at[pl.ds(1, nx - 1)], sem_req.at[1])
    t2[0] = combine(t1, lane // ny, nx)
    for b in range(1, ny):
        send(t2.at[0], t2.at[b], sem_req.at[2], sem_req.at[3], (tx, lax.rem(ty + b, ny)))
    with jax.named_scope("laplace"):
        for i in range(2):
            drain(hrin.at[i], sem_halo.at[i])
            drain(hcin.at[i], sem_halo.at[2 + i])
        below = jnp.where(tx == nx - 1, 0.0, hrin[0])
        above = jnp.where(tx == 0, 0.0, hrin[1])
        right = jnp.where(ty == ny - 1, 0.0, hcin[0])
        left = jnp.where(ty == 0, 0.0, hcin[1])
        side = jnp.where(row < 4, right, left)
        side = jnp.concatenate([side, jnp.zeros((120, 128), F32)], axis=0).T
        row_f = lax.broadcasted_iota(jnp.int32, (rows, cols), 0)
        col_f = lax.broadcasted_iota(jnp.int32, (rows, cols), 1)
        for b in range(beacons):
            d = dir_ref[b]
            up = jnp.where(row_f == 0, above[4 + b : 5 + b], pltpu.roll(d, 1, 0))
            down = jnp.where(row_f == rows - 1, below[b : b + 1], pltpu.roll(d, rows - 1, 0))
            west = jnp.where(col_f == 0, side[:rows, 4 + b : 5 + b], pltpu.roll(d, 1, 1))
            east = jnp.where(col_f == cols - 1, side[:rows, b : b + 1], pltpu.roll(d, cols - 1, 1))
            image_ref[b] = SMOOTH * (4.0 * d - (down + up + east + west))

    drain(t2.at[pl.ds(1, ny - 1)], sem_req.at[3])
    table = combine(t2, lax.rem(lane, ny), ny)
    want_v[...] = jnp.maximum(table, 0.0).astype(jnp.int32)
    want_copy = pltpu.make_async_copy(want_v, want_s, sem_loc.at[1])
    want_copy.start()
    want_copy.wait()

    with jax.named_scope("serve"):

        def serve(g, carry):
            for i in range(GROUP):
                k = g * GROUP + i
                for r in range(CAP):
                    sb[k, r] = own[jnp.clip(want_s[r, k], 0, own.shape[0] - 1)]

                def far():
                    send(sb.at[k], fetched.at[k], sem_send.at[0], sem_dir.at[g], behind(g, i))

                def near():
                    pltpu.make_async_copy(sb.at[k], fetched.at[k], sem_dir.at[g]).start()

                if i == 0:
                    pl.when(g == 0)(near)
                    pl.when(g > 0)(far)
                else:
                    far()
            return carry

        lax.fori_loop(0, groups, serve, 0)

    bins_copy.wait()
    blocks_copy.wait()

    low = row < 4

    def products(g, carry):
        drain(fetched.at[pl.ds(g * GROUP, GROUP)], sem_dir.at[g])
        spots = [(g * GROUP + i // CAP, i % CAP) for i in range(GROUP * CAP)]
        ids = [jnp.clip(bins_s[r, k], 0, count - 1) for k, r in spots]
        picked = []
        for i in range(0, GROUP * CAP, 2):
            (kx, rx), (ky, ry) = spots[i : i + 2]
            x, y = fetched[kx, rx].astype(F32), fetched[ky, ry].astype(F32)
            first = jnp.where(low, x, pltpu.roll(y, 4, 0))
            second = jnp.where(low, pltpu.roll(x, 4, 0), y)
            picked.append(jnp.concatenate([first, second], axis=1).astype(BF16))
        pairs = []
        for i in range(0, GROUP * CAP, 2):
            pair = picked[i // 2]
            x = lax.dot_general(pair, bl[ids[i]], NT, preferred_element_type=F32)
            y = lax.dot_general(pair, bl[ids[i + 1]], NT, preferred_element_type=F32)
            pairs.append(jnp.where(low, x, y).astype(BF16))
        for i in range(0, GROUP * CAP, 2):
            pair = pairs[i // 2]
            x = lax.dot_general(pair, bl[ids[i]], NN, preferred_element_type=F32)
            y = lax.dot_general(pair, bl[ids[i + 1]], NN, preferred_element_type=F32)
            (kx, rx), (ky, ry) = spots[i : i + 2]
            ret[kx, rx] = jnp.where(low, x[:, :128], pltpu.roll(x[:, 128:], 4, 0)).astype(BF16)
            ret[ky, ry] = jnp.where(low, pltpu.roll(y[:, :128], 4, 0), y[:, 128:]).astype(BF16)
        for i in range(GROUP):
            k = g * GROUP + i

            def far():
                send(ret.at[k], arrived.at[k], sem_send.at[1], sem_ret.at[g], ahead(g, i))

            def near():
                pltpu.make_async_copy(ret.at[k], arrived.at[k], sem_ret.at[g]).start()

            if i == 0:
                pl.when(g == 0)(near)
                pl.when(g > 0)(far)
            else:
                far()
        return carry

    with jax.named_scope("products"):
        lax.fori_loop(0, groups, products, 0)

    with jax.named_scope("add_up"):

        def widen(g, carry):
            drain(arrived.at[pl.ds(g * GROUP, GROUP)], sem_ret.at[g])
            for i in range(GROUP):
                for r in range(CAP):
                    at = pl.multiple_of((g * GROUP + i) * 8 * CAP + r * 8, 8)
                    acc_ref[pl.ds(at, 8), :] = arrived[g * GROUP + i, r].astype(F32)
            return carry

        number = lax.broadcasted_iota(jnp.int32, (128, 128), 0).astype(F32)
        split = groups * 3 // 4
        for start, stop in ((0, split), (split, groups)):
            lax.fori_loop(start, stop, widen, 0)
            k0, nk = start * GROUP, (stop - start) * GROUP
            hits = jnp.concatenate(
                [jnp.where(number == table[r : r + 1], 1.0, 0.0).astype(BF16)[:, k0 : k0 + nk] for r in range(CAP)],
                axis=1,
            )
            for j in range(8):
                terms = [acc_ref[pl.ds((k0 * CAP + r) * 8 + j, nk, stride=8 * CAP), :] for r in range(CAP)]
                terms = jnp.concatenate(terms, axis=0).astype(BF16)
                part = lax.dot_general(hits, terms, NN, preferred_element_type=F32)
                if start:
                    part += til[pl.ds(j, 128, stride=8), :]
                til[pl.ds(j, 128, stride=8), :] = part

        def paste(ti, carry):
            for half in range(2):
                regs = []
                for q in range(8):
                    at = pl.multiple_of((ti * 16 + half * 8 + q) * 8, 8)
                    regs.append(til[pl.ds(at, 8), :])
                for r, reg in enumerate(swap_blocks(regs, lane)):
                    fld[half, pl.ds(ti * 64 + r, 8, stride=8), :] = reg
            return carry

        lax.fori_loop(0, rows // SIDE, paste, 0)

    with jax.named_scope("sums"):
        stack = jnp.zeros((16, 128), F32)
        which = lax.broadcasted_iota(jnp.int32, (16, 128), 0)
        spot = lax.broadcasted_iota(jnp.int32, (16, 128), 1) >> 3
        scales = []
        for b in range(beacons):
            top = jnp.max(jnp.where((lane >> 5) == b, jnp.broadcast_to(table[3:4], (8, 128)), 0.0), axis=1, keepdims=True)
            top = jnp.maximum(jnp.broadcast_to(top, (8, 128)), 1e-30)
            scales.append(top)
            inverse = 1.0 / top
            dq = jnp.zeros((8, 128), F32)
            rq = jnp.zeros((8, 128), F32)
            qq = jnp.zeros((8, 128), F32)
            for s in range(rows // 8):
                at = (s // 2) * 64 + (s % 2) * 32 + b * 8
                for half in range(2):
                    span = (b, slice(s * 8, s * 8 + 8), slice(half * 128, half * 128 + 128))
                    q = fld[half, at : at + 8, :] + image_ref[span]
                    image_ref[span] = q
                    dq += dir_ref[span] * q
                    q = q * inverse
                    rq += res_ref[span] * q
                    qq += q * q
            for i, x in enumerate((dq, rq, qq)):
                stack = jnp.where(which == 4 * i + b, jnp.sum(x, axis=0, keepdims=True), stack)
        for shift in (64, 32, 16, 8):
            stack = stack + pltpu.roll(stack, shift, 1)
        s1[0:1, :] = jnp.sum(jnp.where(which == spot, stack, 0.0), axis=0, keepdims=True)

    with jax.named_scope("reduce"):

        def spread(g, carry):
            for i in range(GROUP):

                def far():
                    k = g * GROUP + i
                    send(s1.at[pl.ds(0, 1)], s1.at[pl.ds(k, 1)], sem_red.at[0], sem_red.at[1], ahead(g, i))

                if i == 0:
                    pl.when(g > 0)(far)
                else:
                    far()
            return carry

        lax.fori_loop(0, groups, spread, 0)
        drain(s1.at[pl.ds(1, n - 1)], sem_red.at[1])
        total = jnp.sum(s1[...], axis=0, keepdims=True)
        total = jnp.sum(jnp.where(which == spot, total, 0.0), axis=1, keepdims=True)
        total = jnp.broadcast_to(total, (16, 128))

        def whole(x):
            return jnp.broadcast_to(jnp.sum(x, axis=1, keepdims=True), (8, 128))

        norm_old = pltpu.roll(whole(table), 4, 0)
        curvature = total[:8]
        cross = pltpu.roll(total[:8], 4, 0)
        square = total[8:]
        top = scales[0]
        for b in range(1, beacons):
            top = jnp.where(row == b, scales[b], top)
        alpha = norm_old / curvature
        step = alpha * top
        norm_new = jnp.maximum(norm_old - 2.0 * step * cross + step * step * square, 0.0)
        beta = norm_new / norm_old
        coef_ref[...] = jnp.where(row < 4, alpha, pltpu.roll(beta, 4, 0))

    drain(t1.at[pl.ds(1, nx - 1)], sem_req.at[0])
    drain(t2.at[pl.ds(1, ny - 1)], sem_req.at[2])
    for i in range(2):
        drain(hr, sem_halo.at[4 + i])
        drain(hc, sem_halo.at[6 + i])
    drain(sb.at[pl.ds(1, n - 1)], sem_send.at[0])
    drain(ret.at[pl.ds(1, n - 1)], sem_send.at[1])
    drain(s1.at[pl.ds(1, n - 1)], sem_red.at[0])


def per_device(nx, ny, solution, residual, direction, blocks, bin_owner, bin_tile):
    n = nx * ny
    beacons, rows, cols = direction.shape
    count = blocks.shape[0]
    vmem = pl.BlockSpec(memory_space=pltpu.VMEM)
    groups = n // GROUP
    slots = (n, CAP, 8, 128)
    image, coef = pl.pallas_call(
        functools.partial(kernel, nx, ny),
        out_shape=(
            jax.ShapeDtypeStruct(direction.shape, F32),
            jax.ShapeDtypeStruct((8, 128), F32),
        ),
        in_specs=[pl.BlockSpec(memory_space=pl.ANY)] * 4,
        out_specs=(vmem, vmem),
        scratch_shapes=[
            pltpu.VMEM((1, count), jnp.int32),
            pltpu.VMEM(direction.shape, F32),
            pltpu.VMEM(direction.shape, F32),
            pltpu.VMEM(blocks.shape, BF16),
            pltpu.VMEM((nx, 8, 128), F32),
            pltpu.VMEM((ny, 8, 128), F32),
            pltpu.VMEM((128, 8, 128), BF16),
            pltpu.VMEM(slots, BF16),
            pltpu.VMEM(slots, BF16),
            pltpu.VMEM(slots, BF16),
            pltpu.VMEM(slots, BF16),
            pltpu.VMEM(((n + 1) * CAP * 8, 128), F32),
            pltpu.VMEM((2, beacons * rows + 8, 128), F32),
            pltpu.VMEM((1032, 128), F32),
            pltpu.VMEM((8, cols), F32),
            pltpu.VMEM((2, 8, cols), F32),
            pltpu.VMEM((8, 128), F32),
            pltpu.VMEM((2, 8, 128), F32),
            pltpu.VMEM((8, 128), jnp.int32),
            pltpu.VMEM((8, 128), jnp.int32),
            pltpu.VMEM((n, 128), F32),
            pltpu.SMEM((8, 128), jnp.int32),
            pltpu.SMEM((8, 128), jnp.int32),
            pltpu.SemaphoreType.DMA,
            pltpu.SemaphoreType.DMA((5,)),
            pltpu.SemaphoreType.DMA((4,)),
            pltpu.SemaphoreType.DMA((8,)),
            pltpu.SemaphoreType.DMA((groups,)),
            pltpu.SemaphoreType.DMA((groups,)),
            pltpu.SemaphoreType.DMA((2,)),
            pltpu.SemaphoreType.DMA((2,)),
        ],
        compiler_params=pltpu.CompilerParams(
            collective_id=0, has_side_effects=True, vmem_limit_bytes=53 * 2**20
        ),
        cost_estimate=pl.CostEstimate(
            flops=4 * count * 128 * 256 * 4, bytes_accessed=blocks.size * 2, transcendentals=0
        ),
        name="radio_map",
    )(bin_owner.reshape(1, count) * 128 + bin_tile.reshape(1, count), direction, residual, blocks)
    alpha = coef[:4, 0][:, None, None]
    beta = coef[4:, 0][:, None, None]
    next_residual = residual - alpha * image
    next_solution = solution + alpha * direction
    next_direction = next_residual + beta * direction
    return next_solution, next_residual, next_direction


def solution(mesh):
    field = P(None, "tx", "ty")
    return jax.shard_map(
        functools.partial(per_device, mesh.shape["tx"], mesh.shape["ty"]),
        mesh=mesh,
        in_specs=(field, field, field, P(("tx", "ty"), None, None), P(("tx", "ty"), None), P(("tx", "ty"))),
        out_specs=(field, field, field),
        check_vma=False,
    )
```

```python
import functools

import jax
import jax.numpy as jnp
from jax import lax
from jax.experimental import pallas as pl
from jax.experimental.pallas import tpu as pltpu
from jax.sharding import PartitionSpec as P

SIDE = 16
CAP = 3
GROUP = 8
SMOOTH = 0.25
MESH = pl.DeviceIdType.MESH
F32 = jnp.float32
BF16 = jnp.bfloat16
NT = (((1,), (1,)), ((), ()))
NN = (((1,), (0,)), ((), ()))


def swap_blocks(regs, lane):
    for j in (4, 2, 1):
        low = ((lane >> 4) & j) == 0
        made = list(regs)
        for r in range(8):
            if r & j == 0:
                a, b = regs[r], regs[r + j]
                made[r] = jnp.where(low, a, pltpu.roll(b, 16 * j, 1))
                made[r + j] = jnp.where(low, pltpu.roll(a, 128 - 16 * j, 1), b)
        regs = made
    return regs


def fold(x):
    rows, cols = x.shape
    y = x.reshape(rows // 8, 8, cols).sum(axis=0)
    return sum(y[:, c : c + 128] for c in range(0, cols, 128))


def fold_max(x):
    rows, cols = x.shape
    y = x.reshape(rows // 8, 8, cols).max(axis=0)
    out = y[:, :128]
    for c in range(128, cols, 128):
        out = jnp.maximum(out, y[:, c : c + 128])
    return out


def kernel(
    nx,
    ny,
    owner_hbm,
    tile_hbm,
    dir_hbm,
    res_hbm,
    blocks_ref,
    image_ref,
    coef_ref,
    owner_ref,
    tile_ref,
    dir_ref,
    res_ref,
    bl,
    t1,
    t2,
    own,
    sb,
    fetched,
    ret,
    arrived,
    acc_ref,
    fld,
    til,
    hr,
    hrin,
    hc,
    hcin,
    bins_v,
    want_v,
    s1,
    bins_s,
    want_s,
    sem_bl,
    sem_loc,
    sem_req,
    sem_halo,
    sem_dir,
    sem_ret,
    sem_send,
    sem_red,
):
    n = nx * ny
    beacons, rows, cols = dir_ref.shape
    count = owner_ref.shape[1]
    groups = n // GROUP
    tx, ty = lax.axis_index("tx"), lax.axis_index("ty")

    def place(g, i):
        if ny % GROUP == 0:
            return lax.div(g * GROUP, ny), lax.rem(g * GROUP, ny) + i
        return lax.div(g * GROUP + i, ny), lax.rem(g * GROUP + i, ny)

    def ahead(g, i):
        a, b = place(g, i)
        x, y = tx + a, ty + b
        return jnp.where(x >= nx, x - nx, x), jnp.where(y >= ny, y - ny, y)

    def behind(g, i):
        a, b = place(g, i)
        x, y = tx - a, ty - b
        return jnp.where(x < 0, x + nx, x), jnp.where(y < 0, y + ny, y)

    def send(src, dst, send_sem, recv_sem, device):
        pltpu.make_async_remote_copy(
            src_ref=src,
            dst_ref=dst,
            send_sem=send_sem,
            recv_sem=recv_sem,
            device_id=device,
            device_id_type=MESH,
        ).start()

    def drain(ref, sem):
        pltpu.make_async_copy(ref, ref, sem).wait()

    loads = [
        pltpu.make_async_copy(src, dst, sem_loc.at[2 + i])
        for i, (src, dst) in enumerate(
            ((owner_hbm, owner_ref), (tile_hbm, tile_ref), (dir_hbm, dir_ref), (res_hbm, res_ref))
        )
    ]
    for load in loads:
        load.start()
    blocks_copy = pltpu.make_async_copy(blocks_ref, bl, sem_bl)
    blocks_copy.start()

    barrier = pltpu.get_barrier_semaphore()
    for a in range(1, nx):
        pl.semaphore_signal(barrier, inc=1, device_id=(lax.rem(tx + a, nx), ty), device_id_type=MESH)
    for b in range(1, ny):
        pl.semaphore_signal(barrier, inc=1, device_id=(tx, lax.rem(ty + b, ny)), device_id_type=MESH)

    lane = lax.broadcasted_iota(jnp.int32, (8, 128), 1)
    row = lax.broadcasted_iota(jnp.int32, (8, 128), 0)

    with jax.named_scope("requests"):
        loads[0].wait()
        loads[1].wait()
        owner, tile = owner_ref[...], tile_ref[...]
        ox, oy = owner // ny, lax.rem(owner, ny)
        dx, dy = ox - tx, oy - ty
        rel = jnp.where(dx < 0, dx + nx, dx) * ny + jnp.where(dy < 0, dy + ny, dy)
        member = rel == lax.broadcasted_iota(jnp.int32, (128, count), 0)
        earlier = lax.broadcasted_iota(jnp.int32, (count, count), 0) < lax.broadcasted_iota(
            jnp.int32, (count, count), 1
        )
        before = lax.dot_general(
            member.astype(F32).astype(BF16),
            earlier.astype(F32).astype(BF16),
            NN,
            preferred_element_type=F32,
        )
        told = lax.broadcasted_iota(jnp.int32, (16, count), 0)
        bin_no = lax.broadcasted_iota(jnp.int32, (16, count), 1)
        payload = jnp.where(told < 8, tile + 1, bin_no + 1).astype(F32)
        slots = jnp.zeros((16, 128), F32)
        for r in range(CAP):
            chosen = jnp.where(member, jnp.where(before == float(r), 1.0, 0.0), 0.0).astype(BF16)
            mine = jnp.where((told & 7) == r, payload, 0.0).astype(BF16)
            slots += lax.dot_general(mine, chosen, NT, preferred_element_type=F32)
        slots = slots - 1.0
        bins_v[...] = jnp.maximum(slots[8:], 0.0).astype(jnp.int32)
        bins_copy = pltpu.make_async_copy(bins_v, bins_s, sem_loc.at[0])
        bins_copy.start()

        table = jnp.where(row < CAP, slots[:8], 0.0)
        loads[2].wait()
        loads[3].wait()
        for b in range(beacons):
            norm = jnp.sum(fold(res_ref[b] * res_ref[b]), axis=0, keepdims=True)
            table = jnp.where(row == 4 + b, norm, table)
            high = jnp.max(fold_max(jnp.abs(dir_ref[b])), axis=0, keepdims=True)
            high = jnp.broadcast_to(high, (8, 128))
            high = jnp.maximum(high, pltpu.roll(high, 64, 1))
            high = jnp.maximum(high, pltpu.roll(high, 32, 1))
            table = jnp.where((row == 3) & ((lane >> 5) == b), high, table)
        t1[0] = table

    pl.semaphore_wait(barrier, nx - 1 + ny - 1)

    for a in range(1, nx):
        send(t1.at[0], t1.at[a], sem_req.at[0], sem_req.at[1], (lax.rem(tx + a, nx), ty))

    columns = jnp.zeros((rows, 128), F32)
    lane_r = lax.broadcasted_iota(jnp.int32, (rows, 128), 1)
    for b in range(beacons):
        hr[b : b + 1, :] = dir_ref[b, 0:1, :]
        hr[4 + b : 5 + b, :] = dir_ref[b, rows - 1 : rows, :]
        columns = jnp.where(lane_r == b, dir_ref[b, :, 0:1], columns)
        columns = jnp.where(lane_r == 4 + b, dir_ref[b, :, cols - 1 : cols], columns)
    hc[...] = columns.T[:8]
    send(hr, hrin.at[0], sem_halo.at[4], sem_halo.at[0], (lax.rem(tx + nx - 1, nx), ty))
    send(hr, hrin.at[1], sem_halo.at[5], sem_halo.at[1], (lax.rem(tx + 1, nx), ty))
    send(hc, hcin.at[0], sem_halo.at[6], sem_halo.at[2], (tx, lax.rem(ty + ny - 1, ny)))
    send(hc, hcin.at[1], sem_halo.at[7], sem_halo.at[3], (tx, lax.rem(ty + 1, ny)))

    with jax.named_scope("tiles"):
        for b in range(beacons):
            for s in range(rows // 8):
                at = (s // 2) * 64 + (s % 2) * 32 + b * 8
                for half in range(2):
                    fld[half, at : at + 8, :] = dir_ref[b, s * 8 : s * 8 + 8, half * 128 : half * 128 + 128]

        def cut(ti, carry):
            for half in range(2):
                regs = [fld[half, pl.ds(ti * 64 + r, 8, stride=8), :] for r in range(8)]
                for q, reg in enumerate(swap_blocks(regs, lane)):
                    own[ti * 16 + half * 8 + q] = reg.astype(BF16)
            return carry

        lax.fori_loop(0, rows // SIDE, cut, 0)

    def combine(tables, place, total):
        asked, high, summed = tables[0], tables[0], tables[0]
        for i in range(1, total):
            asked = jnp.where(place == i, tables[i], asked)
            high = jnp.maximum(high, tables[i])
            summed = summed + tables[i]
        return jnp.where(row < CAP, asked, jnp.where(row == CAP, high, summed))

    drain(t1.at[pl.ds(1, nx - 1)], sem_req.at[1])
    t2[0] = combine(t1, lane // ny, nx)
    for b in range(1, ny):
        send(t2.at[0], t2.at[b], sem_req.at[2], sem_req.at[3], (tx, lax.rem(ty + b, ny)))
    with jax.named_scope("laplace"):
        for i in range(2):
            drain(hrin.at[i], sem_halo.at[i])
            drain(hcin.at[i], sem_halo.at[2 + i])
        below = jnp.where(tx == nx - 1, 0.0, hrin[0])
        above = jnp.where(tx == 0, 0.0, hrin[1])
        right = jnp.where(ty == ny - 1, 0.0, hcin[0])
        left = jnp.where(ty == 0, 0.0, hcin[1])
        side = jnp.where(row < 4, right, left)
        side = jnp.concatenate([side, jnp.zeros((120, 128), F32)], axis=0).T
        row_f = lax.broadcasted_iota(jnp.int32, (rows, cols), 0)
        col_f = lax.broadcasted_iota(jnp.int32, (rows, cols), 1)
        for b in range(beacons):
            d = dir_ref[b]
            up = jnp.where(row_f == 0, above[4 + b : 5 + b], pltpu.roll(d, 1, 0))
            down = jnp.where(row_f == rows - 1, below[b : b + 1], pltpu.roll(d, rows - 1, 0))
            west = jnp.where(col_f == 0, side[:rows, 4 + b : 5 + b], pltpu.roll(d, 1, 1))
            east = jnp.where(col_f == cols - 1, side[:rows, b : b + 1], pltpu.roll(d, cols - 1, 1))
            image_ref[b] = SMOOTH * (4.0 * d - (down + up + east + west))

    drain(t2.at[pl.ds(1, ny - 1)], sem_req.at[3])
    table = combine(t2, lax.rem(lane, ny), ny)
    want_v[...] = jnp.maximum(table, 0.0).astype(jnp.int32)
    want_copy = pltpu.make_async_copy(want_v, want_s, sem_loc.at[1])
    want_copy.start()
    want_copy.wait()

    with jax.named_scope("serve"):

        def serve(g, carry):
            for i in range(GROUP):
                k = g * GROUP + i
                for r in range(CAP):
                    sb[k, r] = own[jnp.clip(want_s[r, k], 0, own.shape[0] - 1)]

                def far():
                    send(sb.at[k], fetched.at[k], sem_send.at[0], sem_dir.at[g], behind(g, i))

                def near():
                    pltpu.make_async_copy(sb.at[k], fetched.at[k], sem_dir.at[g]).start()

                if i == 0:
                    pl.when(g == 0)(near)
                    pl.when(g > 0)(far)
                else:
                    far()
            return carry

        lax.fori_loop(0, groups, serve, 0)

    bins_copy.wait()
    blocks_copy.wait()

    low = row < 4

    def products(g, carry):
        drain(fetched.at[pl.ds(g * GROUP, GROUP)], sem_dir.at[g])
        spots = [(g * GROUP + i // CAP, i % CAP) for i in range(GROUP * CAP)]
        ids = [jnp.clip(bins_s[r, k], 0, count - 1) for k, r in spots]
        picked = []
        for i in range(0, GROUP * CAP, 2):
            (kx, rx), (ky, ry) = spots[i : i + 2]
            x, y = fetched[kx, rx].astype(F32), fetched[ky, ry].astype(F32)
            first = jnp.where(low, x, pltpu.roll(y, 4, 0))
            second = jnp.where(low, pltpu.roll(x, 4, 0), y)
            picked.append(jnp.concatenate([first, second], axis=1).astype(BF16))
        pairs = []
        for i in range(0, GROUP * CAP, 2):
            pair = picked[i // 2]
            x = lax.dot_general(pair, bl[ids[i]], NT, preferred_element_type=F32)
            y = lax.dot_general(pair, bl[ids[i + 1]], NT, preferred_element_type=F32)
            pairs.append(jnp.where(low, x, y).astype(BF16))
        for i in range(0, GROUP * CAP, 2):
            pair = pairs[i // 2]
            x = lax.dot_general(pair, bl[ids[i]], NN, preferred_element_type=F32)
            y = lax.dot_general(pair, bl[ids[i + 1]], NN, preferred_element_type=F32)
            (kx, rx), (ky, ry) = spots[i : i + 2]
            ret[kx, rx] = jnp.where(low, x[:, :128], pltpu.roll(x[:, 128:], 4, 0)).astype(BF16)
            ret[ky, ry] = jnp.where(low, pltpu.roll(y[:, :128], 4, 0), y[:, 128:]).astype(BF16)
        for i in range(GROUP):
            k = g * GROUP + i

            def far():
                send(ret.at[k], arrived.at[k], sem_send.at[1], sem_ret.at[g], ahead(g, i))

            def near():
                pltpu.make_async_copy(ret.at[k], arrived.at[k], sem_ret.at[g]).start()

            if i == 0:
                pl.when(g == 0)(near)
                pl.when(g > 0)(far)
            else:
                far()
        return carry

    with jax.named_scope("products"):
        lax.fori_loop(0, groups, products, 0)

    with jax.named_scope("add_up"):

        def widen(g, carry):
            drain(arrived.at[pl.ds(g * GROUP, GROUP)], sem_ret.at[g])
            for i in range(GROUP):
                for r in range(CAP):
                    at = pl.multiple_of((g * GROUP + i) * 8 * CAP + r * 8, 8)
                    acc_ref[pl.ds(at, 8), :] = arrived[g * GROUP + i, r].astype(F32)
            return carry

        number = lax.broadcasted_iota(jnp.int32, (128, 128), 0).astype(F32)
        split = groups * 3 // 4
        for start, stop in ((0, split), (split, groups)):
            lax.fori_loop(start, stop, widen, 0)
            k0, nk = start * GROUP, (stop - start) * GROUP
            hits = jnp.concatenate(
                [jnp.where(number == table[r : r + 1], 1.0, 0.0).astype(BF16)[:, k0 : k0 + nk] for r in range(CAP)],
                axis=1,
            )
            for j in range(8):
                terms = [acc_ref[pl.ds((k0 * CAP + r) * 8 + j, nk, stride=8 * CAP), :] for r in range(CAP)]
                terms = jnp.concatenate(terms, axis=0).astype(BF16)
                part = lax.dot_general(hits, terms, NN, preferred_element_type=F32)
                if start:
                    part += til[pl.ds(j, 128, stride=8), :]
                til[pl.ds(j, 128, stride=8), :] = part

        def paste(ti, carry):
            for half in range(2):
                regs = []
                for q in range(8):
                    at = pl.multiple_of((ti * 16 + half * 8 + q) * 8, 8)
                    regs.append(til[pl.ds(at, 8), :])
                for r, reg in enumerate(swap_blocks(regs, lane)):
                    fld[half, pl.ds(ti * 64 + r, 8, stride=8), :] = reg
            return carry

        lax.fori_loop(0, rows // SIDE, paste, 0)

    with jax.named_scope("sums"):
        stack = jnp.zeros((16, 128), F32)
        which = lax.broadcasted_iota(jnp.int32, (16, 128), 0)
        spot = lax.broadcasted_iota(jnp.int32, (16, 128), 1) >> 3
        scales = []
        for b in range(beacons):
            top = jnp.max(jnp.where((lane >> 5) == b, jnp.broadcast_to(table[3:4], (8, 128)), 0.0), axis=1, keepdims=True)
            top = jnp.maximum(jnp.broadcast_to(top, (8, 128)), 1e-30)
            scales.append(top)
            inverse = 1.0 / top
            dq = jnp.zeros((8, 128), F32)
            rq = jnp.zeros((8, 128), F32)
            qq = jnp.zeros((8, 128), F32)
            for s in range(rows // 8):
                at = (s // 2) * 64 + (s % 2) * 32 + b * 8
                for half in range(2):
                    span = (b, slice(s * 8, s * 8 + 8), slice(half * 128, half * 128 + 128))
                    q = fld[half, at : at + 8, :] + image_ref[span]
                    image_ref[span] = q
                    dq += dir_ref[span] * q
                    q = q * inverse
                    rq += res_ref[span] * q
                    qq += q * q
            for i, x in enumerate((dq, rq, qq)):
                stack = jnp.where(which == 4 * i + b, jnp.sum(x, axis=0, keepdims=True), stack)
        for shift in (64, 32, 16, 8):
            stack = stack + pltpu.roll(stack, shift, 1)
        s1[0:1, :] = jnp.sum(jnp.where(which == spot, stack, 0.0), axis=0, keepdims=True)

    with jax.named_scope("reduce"):

        def spread(g, carry):
            for i in range(GROUP):

                def far():
                    k = g * GROUP + i
                    send(s1.at[pl.ds(0, 1)], s1.at[pl.ds(k, 1)], sem_red.at[0], sem_red.at[1], ahead(g, i))

                if i == 0:
                    pl.when(g > 0)(far)
                else:
                    far()
            return carry

        lax.fori_loop(0, groups, spread, 0)
        drain(s1.at[pl.ds(1, n - 1)], sem_red.at[1])
        total = jnp.sum(s1[...], axis=0, keepdims=True)
        total = jnp.sum(jnp.where(which == spot, total, 0.0), axis=1, keepdims=True)
        total = jnp.broadcast_to(total, (16, 128))

        def whole(x):
            return jnp.broadcast_to(jnp.sum(x, axis=1, keepdims=True), (8, 128))

        norm_old = pltpu.roll(whole(table), 4, 0)
        curvature = total[:8]
        cross = pltpu.roll(total[:8], 4, 0)
        square = total[8:]
        top = scales[0]
        for b in range(1, beacons):
            top = jnp.where(row == b, scales[b], top)
        alpha = norm_old / curvature
        step = alpha * top
        norm_new = jnp.maximum(norm_old - 2.0 * step * cross + step * step * square, 0.0)
        beta = norm_new / norm_old
        coef_ref[...] = jnp.where(row < 4, alpha, pltpu.roll(beta, 4, 0))

    drain(t1.at[pl.ds(1, nx - 1)], sem_req.at[0])
    drain(t2.at[pl.ds(1, ny - 1)], sem_req.at[2])
    for i in range(2):
        drain(hr, sem_halo.at[4 + i])
        drain(hc, sem_halo.at[6 + i])
    drain(sb.at[pl.ds(1, n - 1)], sem_send.at[0])
    drain(ret.at[pl.ds(1, n - 1)], sem_send.at[1])
    drain(s1.at[pl.ds(1, n - 1)], sem_red.at[0])


def per_device(nx, ny, solution, residual, direction, blocks, bin_owner, bin_tile):
    n = nx * ny
    beacons, rows, cols = direction.shape
    count = blocks.shape[0]
    vmem = pl.BlockSpec(memory_space=pltpu.VMEM)
    groups = n // GROUP
    slots = (n, CAP, 8, 128)
    image, coef = pl.pallas_call(
        functools.partial(kernel, nx, ny),
        out_shape=(
            jax.ShapeDtypeStruct(direction.shape, F32),
            jax.ShapeDtypeStruct((8, 128), F32),
        ),
        in_specs=[pl.BlockSpec(memory_space=pl.ANY)] * 5,
        out_specs=(vmem, vmem),
        scratch_shapes=[
            pltpu.VMEM((1, count), jnp.int32),
            pltpu.VMEM((1, count), jnp.int32),
            pltpu.VMEM(direction.shape, F32),
            pltpu.VMEM(direction.shape, F32),
            pltpu.VMEM(blocks.shape, BF16),
            pltpu.VMEM((nx, 8, 128), F32),
            pltpu.VMEM((ny, 8, 128), F32),
            pltpu.VMEM((128, 8, 128), BF16),
            pltpu.VMEM(slots, BF16),
            pltpu.VMEM(slots, BF16),
            pltpu.VMEM(slots, BF16),
            pltpu.VMEM(slots, BF16),
            pltpu.VMEM(((n + 1) * CAP * 8, 128), F32),
            pltpu.VMEM((2, beacons * rows + 8, 128), F32),
            pltpu.VMEM((1032, 128), F32),
            pltpu.VMEM((8, cols), F32),
            pltpu.VMEM((2, 8, cols), F32),
            pltpu.VMEM((8, 128), F32),
            pltpu.VMEM((2, 8, 128), F32),
            pltpu.VMEM((8, 128), jnp.int32),
            pltpu.VMEM((8, 128), jnp.int32),
            pltpu.VMEM((n, 128), F32),
            pltpu.SMEM((8, 128), jnp.int32),
            pltpu.SMEM((8, 128), jnp.int32),
            pltpu.SemaphoreType.DMA,
            pltpu.SemaphoreType.DMA((6,)),
            pltpu.SemaphoreType.DMA((4,)),
            pltpu.SemaphoreType.DMA((8,)),
            pltpu.SemaphoreType.DMA((groups,)),
            pltpu.SemaphoreType.DMA((groups,)),
            pltpu.SemaphoreType.DMA((2,)),
            pltpu.SemaphoreType.DMA((2,)),
        ],
        compiler_params=pltpu.CompilerParams(
            collective_id=0, has_side_effects=True, vmem_limit_bytes=53 * 2**20
        ),
        cost_estimate=pl.CostEstimate(
            flops=4 * count * 128 * 256 * 4, bytes_accessed=blocks.size * 2, transcendentals=0
        ),
        name="radio_map",
    )(
        pltpu.with_memory_space_constraint(bin_owner.reshape(1, count), pltpu.HBM),
        pltpu.with_memory_space_constraint(bin_tile.reshape(1, count), pltpu.HBM),
        direction,
        residual,
        blocks,
    )
    alpha = coef[:4, 0][:, None, None]
    beta = coef[4:, 0][:, None, None]
    next_residual = residual - alpha * image
    next_solution = solution + alpha * direction
    next_direction = next_residual + beta * direction
    return next_solution, next_residual, next_direction


def solution(mesh):
    field = P(None, "tx", "ty")
    return jax.shard_map(
        functools.partial(per_device, mesh.shape["tx"], mesh.shape["ty"]),
        mesh=mesh,
        in_specs=(field, field, field, P(("tx", "ty"), None, None), P(("tx", "ty"), None), P(("tx", "ty"))),
        out_specs=(field, field, field),
        check_vma=False,
    )
```

```python
import functools

import jax
import jax.numpy as jnp
from jax import lax
from jax.experimental import pallas as pl
from jax.experimental.pallas import tpu as pltpu
from jax.sharding import PartitionSpec as P

SIDE = 16
CAP = 3
GROUP = 8
SMOOTH = 0.25
MESH = pl.DeviceIdType.MESH
F32 = jnp.float32
BF16 = jnp.bfloat16
NT = (((1,), (1,)), ((), ()))
NN = (((1,), (0,)), ((), ()))


def swap_blocks(regs, lane):
    for j in (4, 2, 1):
        low = ((lane >> 4) & j) == 0
        made = list(regs)
        for r in range(8):
            if r & j == 0:
                a, b = regs[r], regs[r + j]
                made[r] = jnp.where(low, a, pltpu.roll(b, 16 * j, 1))
                made[r + j] = jnp.where(low, pltpu.roll(a, 128 - 16 * j, 1), b)
        regs = made
    return regs


def fold(x):
    rows, cols = x.shape
    y = x.reshape(rows // 8, 8, cols).sum(axis=0)
    return sum(y[:, c : c + 128] for c in range(0, cols, 128))


def fold_max(x):
    rows, cols = x.shape
    y = x.reshape(rows // 8, 8, cols).max(axis=0)
    out = y[:, :128]
    for c in range(128, cols, 128):
        out = jnp.maximum(out, y[:, c : c + 128])
    return out


def kernel(
    nx,
    ny,
    owner_hbm,
    tile_hbm,
    dir_hbm,
    res_hbm,
    blocks_ref,
    image_ref,
    coef_ref,
    owner_ref,
    tile_ref,
    dir_ref,
    res_ref,
    bl,
    t1,
    t2,
    own,
    sb,
    fetched,
    ret,
    arrived,
    acc_ref,
    fld,
    til,
    hr,
    hrin,
    hc,
    hcin,
    bins_v,
    want_v,
    s1,
    bins_s,
    want_s,
    sem_bl,
    sem_loc,
    sem_req,
    sem_halo,
    sem_dir,
    sem_ret,
    sem_send,
    sem_red,
):
    n = nx * ny
    beacons, rows, cols = dir_ref.shape
    count = owner_ref.shape[1]
    groups = n // GROUP
    tx, ty = lax.axis_index("tx"), lax.axis_index("ty")

    def place(g, i):
        if ny % GROUP == 0:
            return lax.div(g * GROUP, ny), lax.rem(g * GROUP, ny) + i
        return lax.div(g * GROUP + i, ny), lax.rem(g * GROUP + i, ny)

    def ahead(g, i):
        a, b = place(g, i)
        x, y = tx + a, ty + b
        return jnp.where(x >= nx, x - nx, x), jnp.where(y >= ny, y - ny, y)

    def behind(g, i):
        a, b = place(g, i)
        x, y = tx - a, ty - b
        return jnp.where(x < 0, x + nx, x), jnp.where(y < 0, y + ny, y)

    def send(src, dst, send_sem, recv_sem, device):
        pltpu.make_async_remote_copy(
            src_ref=src,
            dst_ref=dst,
            send_sem=send_sem,
            recv_sem=recv_sem,
            device_id=device,
            device_id_type=MESH,
        ).start()

    def drain(ref, sem):
        pltpu.make_async_copy(ref, ref, sem).wait()

    loads = [
        pltpu.make_async_copy(src, dst, sem_loc.at[2 + i])
        for i, (src, dst) in enumerate(
            ((owner_hbm, owner_ref), (tile_hbm, tile_ref), (dir_hbm, dir_ref), (res_hbm, res_ref))
        )
    ]
    for load in loads:
        load.start()
    blocks_copy = pltpu.make_async_copy(blocks_ref, bl, sem_bl)
    blocks_copy.start()

    barrier = pltpu.get_barrier_semaphore()
    for a in range(1, nx):
        pl.semaphore_signal(barrier, inc=1, device_id=(lax.rem(tx + a, nx), ty), device_id_type=MESH)
    for b in range(1, ny):
        pl.semaphore_signal(barrier, inc=1, device_id=(tx, lax.rem(ty + b, ny)), device_id_type=MESH)

    lane = lax.broadcasted_iota(jnp.int32, (8, 128), 1)
    row = lax.broadcasted_iota(jnp.int32, (8, 128), 0)

    with jax.named_scope("requests"):
        loads[0].wait()
        loads[1].wait()
        owner, tile = owner_ref[...], tile_ref[...]
        ox, oy = owner // ny, lax.rem(owner, ny)
        dx, dy = ox - tx, oy - ty
        rel = jnp.where(dx < 0, dx + nx, dx) * ny + jnp.where(dy < 0, dy + ny, dy)
        member = rel == lax.broadcasted_iota(jnp.int32, (128, count), 0)
        earlier = lax.broadcasted_iota(jnp.int32, (count, count), 0) < lax.broadcasted_iota(
            jnp.int32, (count, count), 1
        )
        before = lax.dot_general(
            member.astype(F32).astype(BF16),
            earlier.astype(F32).astype(BF16),
            NN,
            preferred_element_type=F32,
        )
        told = lax.broadcasted_iota(jnp.int32, (16, count), 0)
        bin_no = lax.broadcasted_iota(jnp.int32, (16, count), 1)
        payload = jnp.where(told < 8, tile + 1, bin_no + 1).astype(F32)
        slots = jnp.zeros((16, 128), F32)
        for r in range(CAP):
            chosen = jnp.where(member, jnp.where(before == float(r), 1.0, 0.0), 0.0).astype(BF16)
            mine = jnp.where((told & 7) == r, payload, 0.0).astype(BF16)
            slots += lax.dot_general(mine, chosen, NT, preferred_element_type=F32)
        slots = slots - 1.0
        bins_v[...] = jnp.maximum(slots[8:], 0.0).astype(jnp.int32)
        bins_copy = pltpu.make_async_copy(bins_v, bins_s, sem_loc.at[0])
        bins_copy.start()

        table = jnp.where(row < CAP, slots[:8], 0.0)
        loads[2].wait()
        loads[3].wait()
        for b in range(beacons):
            norm = jnp.sum(fold(res_ref[b] * res_ref[b]), axis=0, keepdims=True)
            table = jnp.where(row == 4 + b, norm, table)
            high = jnp.max(fold_max(jnp.abs(dir_ref[b])), axis=0, keepdims=True)
            high = jnp.broadcast_to(high, (8, 128))
            high = jnp.maximum(high, pltpu.roll(high, 64, 1))
            high = jnp.maximum(high, pltpu.roll(high, 32, 1))
            table = jnp.where((row == 3) & ((lane >> 5) == b), high, table)
        t2[0] = table

    pl.semaphore_wait(barrier, nx - 1 + ny - 1)

    for b in range(1, ny):
        send(t2.at[0], t2.at[b], sem_req.at[0], sem_req.at[1], (tx, lax.rem(ty + b, ny)))

    columns = jnp.zeros((rows, 128), F32)
    lane_r = lax.broadcasted_iota(jnp.int32, (rows, 128), 1)
    for b in range(beacons):
        hr[b : b + 1, :] = dir_ref[b, 0:1, :]
        hr[4 + b : 5 + b, :] = dir_ref[b, rows - 1 : rows, :]
        columns = jnp.where(lane_r == b, dir_ref[b, :, 0:1], columns)
        columns = jnp.where(lane_r == 4 + b, dir_ref[b, :, cols - 1 : cols], columns)
    hc[...] = columns.T[:8]
    send(hr, hrin.at[0], sem_halo.at[4], sem_halo.at[0], (lax.rem(tx + nx - 1, nx), ty))
    send(hr, hrin.at[1], sem_halo.at[5], sem_halo.at[1], (lax.rem(tx + 1, nx), ty))
    send(hc, hcin.at[0], sem_halo.at[6], sem_halo.at[2], (tx, lax.rem(ty + ny - 1, ny)))
    send(hc, hcin.at[1], sem_halo.at[7], sem_halo.at[3], (tx, lax.rem(ty + 1, ny)))

    with jax.named_scope("tiles"):
        for b in range(beacons):
            for s in range(rows // 8):
                at = (s // 2) * 64 + (s % 2) * 32 + b * 8
                for half in range(2):
                    fld[half, at : at + 8, :] = dir_ref[b, s * 8 : s * 8 + 8, half * 128 : half * 128 + 128]

        def cut(ti, carry):
            for half in range(2):
                regs = [fld[half, pl.ds(ti * 64 + r, 8, stride=8), :] for r in range(8)]
                for q, reg in enumerate(swap_blocks(regs, lane)):
                    own[ti * 16 + half * 8 + q] = reg.astype(BF16)
            return carry

        lax.fori_loop(0, rows // SIDE, cut, 0)

    def combine(tables, place, total):
        asked, high, summed = tables[0], tables[0], tables[0]
        for i in range(1, total):
            asked = jnp.where(place == i, tables[i], asked)
            high = jnp.maximum(high, tables[i])
            summed = summed + tables[i]
        return jnp.where(row < CAP, asked, jnp.where(row == CAP, high, summed))

    def serve(which, start, stop):
        def group(g, carry):
            for i in range(GROUP):
                k = g * GROUP + i
                for r in range(CAP):
                    sb[k, r] = own[jnp.clip(want_s[which, r, k], 0, own.shape[0] - 1)]

                def far():
                    send(sb.at[k], fetched.at[k], sem_send.at[0], sem_dir.at[g], behind(g, i))

                def near():
                    pltpu.make_async_copy(sb.at[k], fetched.at[k], sem_dir.at[g]).start()

                if i == 0:
                    pl.when(g == 0)(near)
                    pl.when(g > 0)(far)
                else:
                    far()
            return carry

        lax.fori_loop(start, stop, group, 0)

    def wanted(which, asked):
        want_v[which] = jnp.maximum(asked, 0.0).astype(jnp.int32)
        copy = pltpu.make_async_copy(want_v.at[which], want_s.at[which], sem_loc.at[1])
        copy.start()
        copy.wait()

    early = ny // GROUP
    drain(t2.at[pl.ds(1, ny - 1)], sem_req.at[1])
    t1[0] = combine(t2, lax.rem(lane, ny), ny)
    for a in range(1, nx):
        send(t1.at[0], t1.at[a], sem_req.at[2], sem_req.at[3], (lax.rem(tx + a, nx), ty))
    if early:
        wanted(0, t1[0])
        serve(0, 0, early)
    with jax.named_scope("laplace"):
        for i in range(2):
            drain(hrin.at[i], sem_halo.at[i])
            drain(hcin.at[i], sem_halo.at[2 + i])
        below = jnp.where(tx == nx - 1, 0.0, hrin[0])
        above = jnp.where(tx == 0, 0.0, hrin[1])
        right = jnp.where(ty == ny - 1, 0.0, hcin[0])
        left = jnp.where(ty == 0, 0.0, hcin[1])
        side = jnp.where(row < 4, right, left)
        side = jnp.concatenate([side, jnp.zeros((120, 128), F32)], axis=0).T
        row_f = lax.broadcasted_iota(jnp.int32, (rows, cols), 0)
        col_f = lax.broadcasted_iota(jnp.int32, (rows, cols), 1)
        for b in range(beacons):
            d = dir_ref[b]
            up = jnp.where(row_f == 0, above[4 + b : 5 + b], pltpu.roll(d, 1, 0))
            down = jnp.where(row_f == rows - 1, below[b : b + 1], pltpu.roll(d, rows - 1, 0))
            west = jnp.where(col_f == 0, side[:rows, 4 + b : 5 + b], pltpu.roll(d, 1, 1))
            east = jnp.where(col_f == cols - 1, side[:rows, b : b + 1], pltpu.roll(d, cols - 1, 1))
            image_ref[b] = SMOOTH * (4.0 * d - (down + up + east + west))

    drain(t1.at[pl.ds(1, nx - 1)], sem_req.at[3])
    table = combine(t1, lane // ny, nx)
    wanted(1, table)
    serve(1, early, groups)

    bins_copy.wait()
    blocks_copy.wait()

    low = row < 4

    def products(g, carry):
        drain(fetched.at[pl.ds(g * GROUP, GROUP)], sem_dir.at[g])
        spots = [(g * GROUP + i // CAP, i % CAP) for i in range(GROUP * CAP)]
        ids = [jnp.clip(bins_s[r, k], 0, count - 1) for k, r in spots]
        picked = []
        for i in range(0, GROUP * CAP, 2):
            (kx, rx), (ky, ry) = spots[i : i + 2]
            x, y = fetched[kx, rx].astype(F32), fetched[ky, ry].astype(F32)
            first = jnp.where(low, x, pltpu.roll(y, 4, 0))
            second = jnp.where(low, pltpu.roll(x, 4, 0), y)
            picked.append(jnp.concatenate([first, second], axis=1).astype(BF16))
        pairs = []
        for i in range(0, GROUP * CAP, 2):
            pair = picked[i // 2]
            x = lax.dot_general(pair, bl[ids[i]], NT, preferred_element_type=F32)
            y = lax.dot_general(pair, bl[ids[i + 1]], NT, preferred_element_type=F32)
            pairs.append(jnp.where(low, x, y).astype(BF16))
        for i in range(0, GROUP * CAP, 2):
            pair = pairs[i // 2]
            x = lax.dot_general(pair, bl[ids[i]], NN, preferred_element_type=F32)
            y = lax.dot_general(pair, bl[ids[i + 1]], NN, preferred_element_type=F32)
            (kx, rx), (ky, ry) = spots[i : i + 2]
            ret[kx, rx] = jnp.where(low, x[:, :128], pltpu.roll(x[:, 128:], 4, 0)).astype(BF16)
            ret[ky, ry] = jnp.where(low, pltpu.roll(y[:, :128], 4, 0), y[:, 128:]).astype(BF16)
        for i in range(GROUP):
            k = g * GROUP + i

            def far():
                send(ret.at[k], arrived.at[k], sem_send.at[1], sem_ret.at[g], ahead(g, i))

            def near():
                pltpu.make_async_copy(ret.at[k], arrived.at[k], sem_ret.at[g]).start()

            if i == 0:
                pl.when(g == 0)(near)
                pl.when(g > 0)(far)
            else:
                far()
        return carry

    with jax.named_scope("products"):
        lax.fori_loop(0, groups, products, 0)

    with jax.named_scope("add_up"):

        def widen(g, carry):
            drain(arrived.at[pl.ds(g * GROUP, GROUP)], sem_ret.at[g])
            for i in range(GROUP):
                for r in range(CAP):
                    at = pl.multiple_of((g * GROUP + i) * 8 * CAP + r * 8, 8)
                    acc_ref[pl.ds(at, 8), :] = arrived[g * GROUP + i, r].astype(F32)
            return carry

        number = lax.broadcasted_iota(jnp.int32, (128, 128), 0).astype(F32)
        split = groups * 3 // 4
        for start, stop in ((0, split), (split, groups)):
            lax.fori_loop(start, stop, widen, 0)
            k0, nk = start * GROUP, (stop - start) * GROUP
            hits = jnp.concatenate(
                [jnp.where(number == table[r : r + 1], 1.0, 0.0).astype(BF16)[:, k0 : k0 + nk] for r in range(CAP)],
                axis=1,
            )
            for j in range(8):
                terms = [acc_ref[pl.ds((k0 * CAP + r) * 8 + j, nk, stride=8 * CAP), :] for r in range(CAP)]
                terms = jnp.concatenate(terms, axis=0).astype(BF16)
                part = lax.dot_general(hits, terms, NN, preferred_element_type=F32)
                if start:
                    part += til[pl.ds(j, 128, stride=8), :]
                til[pl.ds(j, 128, stride=8), :] = part

        def paste(ti, carry):
            for half in range(2):
                regs = []
                for q in range(8):
                    at = pl.multiple_of((ti * 16 + half * 8 + q) * 8, 8)
                    regs.append(til[pl.ds(at, 8), :])
                for r, reg in enumerate(swap_blocks(regs, lane)):
                    fld[half, pl.ds(ti * 64 + r, 8, stride=8), :] = reg
            return carry

        lax.fori_loop(0, rows // SIDE, paste, 0)

    with jax.named_scope("sums"):
        stack = jnp.zeros((16, 128), F32)
        which = lax.broadcasted_iota(jnp.int32, (16, 128), 0)
        spot = lax.broadcasted_iota(jnp.int32, (16, 128), 1) >> 3
        scales = []
        for b in range(beacons):
            top = jnp.max(jnp.where((lane >> 5) == b, jnp.broadcast_to(table[3:4], (8, 128)), 0.0), axis=1, keepdims=True)
            top = jnp.maximum(jnp.broadcast_to(top, (8, 128)), 1e-30)
            scales.append(top)
            inverse = 1.0 / top
            dq = jnp.zeros((8, 128), F32)
            rq = jnp.zeros((8, 128), F32)
            qq = jnp.zeros((8, 128), F32)
            for s in range(rows // 8):
                at = (s // 2) * 64 + (s % 2) * 32 + b * 8
                for half in range(2):
                    span = (b, slice(s * 8, s * 8 + 8), slice(half * 128, half * 128 + 128))
                    q = fld[half, at : at + 8, :] + image_ref[span]
                    image_ref[span] = q
                    dq += dir_ref[span] * q
                    q = q * inverse
                    rq += res_ref[span] * q
                    qq += q * q
            for i, x in enumerate((dq, rq, qq)):
                stack = jnp.where(which == 4 * i + b, jnp.sum(x, axis=0, keepdims=True), stack)
        for shift in (64, 32, 16, 8):
            stack = stack + pltpu.roll(stack, shift, 1)
        s1[0:1, :] = jnp.sum(jnp.where(which == spot, stack, 0.0), axis=0, keepdims=True)

    with jax.named_scope("reduce"):

        def spread(g, carry):
            for i in range(GROUP):

                def far():
                    k = g * GROUP + i
                    send(s1.at[pl.ds(0, 1)], s1.at[pl.ds(k, 1)], sem_red.at[0], sem_red.at[1], ahead(g, i))

                if i == 0:
                    pl.when(g > 0)(far)
                else:
                    far()
            return carry

        lax.fori_loop(0, groups, spread, 0)
        drain(s1.at[pl.ds(1, n - 1)], sem_red.at[1])
        total = jnp.sum(s1[...], axis=0, keepdims=True)
        total = jnp.sum(jnp.where(which == spot, total, 0.0), axis=1, keepdims=True)
        total = jnp.broadcast_to(total, (16, 128))

        def whole(x):
            return jnp.broadcast_to(jnp.sum(x, axis=1, keepdims=True), (8, 128))

        norm_old = pltpu.roll(whole(table), 4, 0)
        curvature = total[:8]
        cross = pltpu.roll(total[:8], 4, 0)
        square = total[8:]
        top = scales[0]
        for b in range(1, beacons):
            top = jnp.where(row == b, scales[b], top)
        alpha = norm_old / curvature
        step = alpha * top
        norm_new = jnp.maximum(norm_old - 2.0 * step * cross + step * step * square, 0.0)
        beta = norm_new / norm_old
        coef_ref[...] = jnp.where(row < 4, alpha, pltpu.roll(beta, 4, 0))

    drain(t2.at[pl.ds(1, ny - 1)], sem_req.at[0])
    drain(t1.at[pl.ds(1, nx - 1)], sem_req.at[2])
    for i in range(2):
        drain(hr, sem_halo.at[4 + i])
        drain(hc, sem_halo.at[6 + i])
    drain(sb.at[pl.ds(1, n - 1)], sem_send.at[0])
    drain(ret.at[pl.ds(1, n - 1)], sem_send.at[1])
    drain(s1.at[pl.ds(1, n - 1)], sem_red.at[0])


def per_device(nx, ny, solution, residual, direction, blocks, bin_owner, bin_tile):
    n = nx * ny
    beacons, rows, cols = direction.shape
    count = blocks.shape[0]
    vmem = pl.BlockSpec(memory_space=pltpu.VMEM)
    groups = n // GROUP
    slots = (n, CAP, 8, 128)
    image, coef = pl.pallas_call(
        functools.partial(kernel, nx, ny),
        out_shape=(
            jax.ShapeDtypeStruct(direction.shape, F32),
            jax.ShapeDtypeStruct((8, 128), F32),
        ),
        in_specs=[pl.BlockSpec(memory_space=pl.ANY)] * 5,
        out_specs=(vmem, vmem),
        scratch_shapes=[
            pltpu.VMEM((1, count), jnp.int32),
            pltpu.VMEM((1, count), jnp.int32),
            pltpu.VMEM(direction.shape, F32),
            pltpu.VMEM(direction.shape, F32),
            pltpu.VMEM(blocks.shape, BF16),
            pltpu.VMEM((nx, 8, 128), F32),
            pltpu.VMEM((ny, 8, 128), F32),
            pltpu.VMEM((128, 8, 128), BF16),
            pltpu.VMEM(slots, BF16),
            pltpu.VMEM(slots, BF16),
            pltpu.VMEM(slots, BF16),
            pltpu.VMEM(slots, BF16),
            pltpu.VMEM(((n + 1) * CAP * 8, 128), F32),
            pltpu.VMEM((2, beacons * rows + 8, 128), F32),
            pltpu.VMEM((1032, 128), F32),
            pltpu.VMEM((8, cols), F32),
            pltpu.VMEM((2, 8, cols), F32),
            pltpu.VMEM((8, 128), F32),
            pltpu.VMEM((2, 8, 128), F32),
            pltpu.VMEM((8, 128), jnp.int32),
            pltpu.VMEM((2, 8, 128), jnp.int32),
            pltpu.VMEM((n, 128), F32),
            pltpu.SMEM((8, 128), jnp.int32),
            pltpu.SMEM((2, 8, 128), jnp.int32),
            pltpu.SemaphoreType.DMA,
            pltpu.SemaphoreType.DMA((6,)),
            pltpu.SemaphoreType.DMA((4,)),
            pltpu.SemaphoreType.DMA((8,)),
            pltpu.SemaphoreType.DMA((groups,)),
            pltpu.SemaphoreType.DMA((groups,)),
            pltpu.SemaphoreType.DMA((2,)),
            pltpu.SemaphoreType.DMA((2,)),
        ],
        compiler_params=pltpu.CompilerParams(
            collective_id=0, has_side_effects=True, vmem_limit_bytes=53 * 2**20
        ),
        cost_estimate=pl.CostEstimate(
            flops=4 * count * 128 * 256 * 4, bytes_accessed=blocks.size * 2, transcendentals=0
        ),
        name="radio_map",
    )(
        pltpu.with_memory_space_constraint(bin_owner.reshape(1, count), pltpu.HBM),
        pltpu.with_memory_space_constraint(bin_tile.reshape(1, count), pltpu.HBM),
        direction,
        residual,
        blocks,
    )
    alpha = coef[:4, 0][:, None, None]
    beta = coef[4:, 0][:, None, None]
    next_residual = residual - alpha * image
    next_solution = solution + alpha * direction
    next_direction = next_residual + beta * direction
    return next_solution, next_residual, next_direction


def solution(mesh):
    field = P(None, "tx", "ty")
    return jax.shard_map(
        functools.partial(per_device, mesh.shape["tx"], mesh.shape["ty"]),
        mesh=mesh,
        in_specs=(field, field, field, P(("tx", "ty"), None, None), P(("tx", "ty"), None), P(("tx", "ty"))),
        out_specs=(field, field, field),
        check_vma=False,
    )
```
